32 devices in a mesh: sub: 8 (over z, x), nar: 4 (over y, core).
Axes of the slice: x: 2, y: 2, z: 4, core: 2. Of those that a mesh axis runs over, the one named last changes fastest.
Arguments:
- remainder_inverse: bfloat16 [32, 2048, 2048], P(('sub', 'nar')), may hold values from -4 to 40, as said below
- dirichlet_schur: bfloat16 [32, 2048, 2048], P(('sub', 'nar')), may hold values from -4 to 40, as said below
- corner_coupling: bfloat16 [32, 24, 2048], P(('sub', 'nar')), may hold values from -0.125 to 0.125
- coarse_inverse: float32 [192, 192], replicated, may hold values from -4 to 40, as said below
- jump_load: float32 [26880, 256], P(('sub', 'nar')), may hold values from -40 to 40
- dof_multiplier: int32 [32, 2048], P(('sub', 'nar')), may hold values from 0 to 26879, as said below
- dof_sign: int32 [32, 2048], P(('sub', 'nar')), may hold values from -1 to 1
- corner_index: int32 [32, 24], P(('sub', 'nar')), may hold values from 0 to 191, as said below
Outputs:
- multipliers: float32 [26880, 256], P(('sub', 'nar'))
- residual: float32 [26880, 256], P(('sub', 'nar'))
The draws below stay inside these ranges and needn't reach their ends.
Inputs may be any that keep to these rules, and one draw needn't show every extreme that they name: Row m of the multipliers belongs to subdomain m // 840 and is named by exactly two entries of dof_multiplier: one in that subdomain's row and one in the row of another subdomain, with opposite nonzero signs in dof_sign. Writing a subdomain as 4 a + b, the other one is 4 a' + b' with a' one of a - 1, a, a + 1 modulo 32 // 4. An entry whose sign is 0 names no multiplier and holds 840 s for its subdomain s. Of one subdomain's 840 rows, the numbers held jointly with each of its 11 partners are, in an order drawn from the seed, 96 five times, 72 three times and 48 three times. `corner_index`: the 24 entries of one subdomain are distinct. `remainder_inverse`: each subdomain's matrix is symmetric positive definite. `dirichlet_schur`: each subdomain's matrix is symmetric positive definite. `coarse_inverse`: symmetric positive definite.
All inputs are finite; a program needn't handle non-finite values.
Results may differ from the reference program's by a relative error of at most 0.012.
The reference program's roundings to bfloat16 on the way count: a program that leaves them out, or rounds other values in their place, can miss the bound.
Values may be sent and summed in bfloat16 or wider, within the bound.
A program may use at most 128 MiB of HBM per device.

```python
import jax
import jax.numpy as jnp
from jax import lax

NR = 2048
NCL = 24
CAP = 96
R = 256
ITERS = 2
SUBS = 32
NL_DEV = 840
NL = 26880
NCG = 192


def definite_block(seed_key, order, lowest, highest, spread):
    noise = jnp.clip(jax.random.normal(seed_key, (order, order), jnp.float32), -6.0, 6.0) * (spread / jnp.sqrt(jnp.float32(order)))
    symmetric = (noise + noise.T) * jnp.sqrt(jnp.float32(0.5))
    diagonal = jax.random.uniform(jax.random.fold_in(seed_key, 1), (order,), jnp.float32, lowest, highest)
    matrix = symmetric + jnp.diag(diagonal)
    return matrix


def draw_remainder_inverse(key, part):
    blocks = lax.map(lambda subdomain: definite_block(jax.random.fold_in(key, subdomain), NR, 1.0, 2.0, 0.4), jnp.arange(SUBS))
    return blocks.astype(jnp.bfloat16)


def draw_dirichlet_schur(key, part):
    blocks = lax.map(lambda subdomain: definite_block(jax.random.fold_in(key, subdomain + 100000), NR, 2.0, 4.0, 0.4), jnp.arange(SUBS))
    return blocks.astype(jnp.bfloat16)


def draw_coarse_inverse(key, part):
    return definite_block(jax.random.fold_in(key, 5), NCG, 2.0, 4.0, 0.5).astype(jnp.float32)


def draw_jump_load(key, part):
    base = jnp.clip(jax.random.normal(jax.random.fold_in(key, 21), (NL, R), jnp.float32), -6.0, 6.0)
    rise_base = 3.0
    column_scale = jnp.exp(jax.random.uniform(jax.random.fold_in(key, 22), (R,), jnp.float32, -1.15, 1.15))
    device_row = (jnp.arange(NL) // NL_DEV).astype(jnp.float32)
    fraction = device_row / jnp.float32(SUBS - 1) - 0.5
    rise = jnp.power(jnp.float32(rise_base), fraction)
    values = base * column_scale[None, :] * rise[:, None]
    return values.astype(jnp.float32)


def build_routing(seed_key):
    count_sub = SUBS // 4
    base_counts = jnp.array([CAP] * 5 + [3 * CAP // 4] * 3 + [CAP // 2] * 3, jnp.int32)
    subdomain = jnp.arange(SUBS, dtype=jnp.int32)
    order_keys = jax.random.split(jax.random.fold_in(seed_key, 1), SUBS)
    chosen = jax.vmap(lambda one_key: jax.random.permutation(one_key, 11).astype(jnp.int32))(order_keys)
    counts = base_counts[chosen]
    peer_rank = jnp.arange(11, dtype=jnp.int32)[None, :]
    classes = peer_rank + (peer_rank >= (4 + subdomain % 4)[:, None]).astype(jnp.int32)
    peers = (subdomain[:, None] // 4 + classes // 4 - 1) % count_sub * 4 + classes % 4
    bounds = jnp.cumsum(counts, axis=1)
    position = jnp.arange(NL_DEV, dtype=jnp.int32)
    peer_slot = jnp.sum((position[None, :, None] >= bounds[:, None, :]).astype(jnp.int32), axis=2)
    shuffle_keys = jax.random.split(jax.random.fold_in(seed_key, 2), SUBS)
    shuffled = jax.vmap(lambda one_key, row_slots: row_slots[jax.random.permutation(one_key, NL_DEV).astype(jnp.int32)])(shuffle_keys, peer_slot)
    partner = jnp.take_along_axis(peers, shuffled, axis=1).reshape(-1).astype(jnp.int32)
    owner_sign = (2 * jax.random.randint(jax.random.fold_in(seed_key, 3), (SUBS * NL_DEV,), 0, 2) - 1).astype(jnp.int32)
    sorter = jnp.argsort(partner, stable=True).astype(jnp.int32)
    sorted_partner = partner[sorter]
    starts = jnp.searchsorted(sorted_partner, subdomain).astype(jnp.int32)
    arrival = jnp.zeros_like(partner).at[sorter].set(jnp.arange(SUBS * NL_DEV, dtype=jnp.int32) - starts[sorted_partner])
    dof_keys = jax.random.split(jax.random.fold_in(seed_key, 4), SUBS)
    layout = jax.vmap(lambda one_key: jax.random.permutation(one_key, NR).astype(jnp.int32))(dof_keys)
    multiplier = jnp.arange(SUBS * NL_DEV, dtype=jnp.int32)
    holder = multiplier // NL_DEV
    own_place = holder * NR + layout[holder, multiplier % NL_DEV]
    far_place = partner * NR + layout[partner, NL_DEV + arrival]
    targets = jnp.repeat(subdomain * NL_DEV, NR).at[own_place].set(multiplier).at[far_place].set(multiplier)
    signs = jnp.zeros((SUBS * NR,), jnp.int32).at[own_place].set(owner_sign).at[far_place].set(-owner_sign)
    return (targets.reshape(SUBS, NR).astype(jnp.int32), signs.reshape(SUBS, NR).astype(jnp.int32))


def draw_dof_multiplier(key, part):
    return build_routing(jax.random.fold_in(key, 7))[0]


def draw_dof_sign(key, part):
    return build_routing(jax.random.fold_in(key, 7))[1]


def draw_corner_index(key, part):
    row_keys = jax.random.split(jax.random.fold_in(key, 9), SUBS)
    picks = jax.vmap(lambda one_key: jax.random.permutation(one_key, NCG)[:NCL].astype(jnp.int32))(row_keys)
    return picks.astype(jnp.int32)


def steps_of(rng, shape, pieces, smallest, high):
    def one(dim, blocks):
        draws = jax.random.uniform(jax.random.fold_in(jax.random.fold_in(rng, 6), dim), (blocks,), jnp.float32, smallest / len(pieces), high / len(pieces))
        return jnp.repeat(jnp.exp(draws), shape[dim] // blocks).reshape((-1,) + (1,) * (len(shape) - dim - 1))

    level = one(*pieces[0])
    for cut in pieces[1:]:
        level = level * one(*cut)
    return level


def scatter_about(stream_key, shape, deviation, most, shards=(), kind=jnp.bfloat16):
    loudness = steps_of(stream_key, shape, shards, -0.22, 0.18) if shards else 1.0
    entries = jax.random.normal(stream_key, shape, jnp.float32) * deviation * loudness
    return jnp.minimum(jnp.maximum(entries, -most), most).astype(kind)


def setup_inputs(seed: int = 0) -> dict:
    keys = jax.random.split(jax.random.key(seed), 9)
    remainder_inverse = draw_remainder_inverse(jax.random.fold_in(keys[8], 71), 0)
    dirichlet_schur = draw_dirichlet_schur(jax.random.fold_in(keys[8], 71), 0)
    corner_coupling = scatter_about(keys[2], (SUBS, NCL, NR), NR ** -0.5, 0.125, ((0, 32),))
    coarse_inverse = draw_coarse_inverse(jax.random.fold_in(keys[8], 71), 0)
    jump_load = draw_jump_load(jax.random.fold_in(keys[8], 71), 0)
    dof_multiplier = draw_dof_multiplier(jax.random.fold_in(keys[8], 71), 0)
    dof_sign = draw_dof_sign(jax.random.fold_in(keys[8], 71), 0)
    corner_index = draw_corner_index(jax.random.fold_in(keys[8], 71), 0)
    return dict(remainder_inverse=remainder_inverse, dirichlet_schur=dirichlet_schur, corner_coupling=corner_coupling, coarse_inverse=coarse_inverse, jump_load=jump_load, dof_multiplier=dof_multiplier, dof_sign=dof_sign, corner_index=corner_index)


def signed_rows(vector, dof_multiplier, dof_sign):
    picked = vector[dof_multiplier] * dof_sign.astype(jnp.float32)[:, :, None]
    return picked.astype(jnp.bfloat16)


def signed_sum(terms, dof_multiplier, dof_sign, row_count):
    weighted = terms.astype(jnp.float32) * dof_sign.astype(jnp.float32)[:, :, None]
    width_cols = terms.shape[2]
    return jnp.zeros((row_count, width_cols), jnp.float32).at[dof_multiplier.reshape(-1)].add(weighted.reshape(-1, width_cols))


def each_product(matrices, operands):
    return lax.map(lambda paired: jnp.dot(paired[0], paired[1], preferred_element_type=jnp.float32), (matrices, operands))


def each_transposed(matrices, operands):
    return lax.map(lambda paired: jnp.dot(paired[0].T, paired[1], preferred_element_type=jnp.float32), (matrices, operands))


def reference(remainder_inverse, dirichlet_schur, corner_coupling, coarse_inverse, jump_load, dof_multiplier, dof_sign, corner_index):
    row_count = jump_load.shape[0]
    columns = jump_load.shape[1]

    def flexibility(vector):
        jumped = signed_rows(vector, dof_multiplier, dof_sign)
        local_part = each_product(remainder_inverse, jumped)
        corner_part = each_product(corner_coupling, jumped)
        coarse_load = jnp.zeros((NCG, columns), jnp.float32).at[corner_index.reshape(-1)].add(corner_part.reshape(-1, columns))
        picked = coarse_inverse[corner_index]
        coarse_solution = jnp.einsum("snc,cr->snr", picked, coarse_load, precision=lax.Precision.HIGHEST).astype(jnp.bfloat16)
        summed = (local_part + each_transposed(corner_coupling, coarse_solution)).astype(jnp.bfloat16)
        return signed_sum(summed, dof_multiplier, dof_sign, row_count)

    def precondition(vector):
        jumped = signed_rows(vector, dof_multiplier, dof_sign)
        stiff_rows = each_product(dirichlet_schur, jumped).astype(jnp.bfloat16)
        return signed_sum(stiff_rows, dof_multiplier, dof_sign, row_count)

    residual = jump_load
    multipliers = jnp.zeros_like(jump_load)
    reduced = precondition(residual)
    energy = jnp.sum(residual * reduced, axis=0)
    direction = reduced
    for iteration in range(ITERS):
        product_rows = flexibility(direction)
        step_size = energy / jnp.sum(direction * product_rows, axis=0)
        multipliers = multipliers + step_size * direction
        residual = residual - step_size * product_rows
        if iteration + 1 < ITERS:
            reduced = precondition(residual)
            energy_later = jnp.sum(residual * reduced, axis=0)
            direction = reduced + (energy_later / energy) * direction
            energy = energy_later
    return multipliers, residual
```

```python
import functools

import jax
import jax.numpy as jnp
from jax import lax
from jax.experimental import pallas as pl
from jax.experimental.pallas import tpu as pltpu
from jax.sharding import PartitionSpec as P

CAP = 96
ITERS = 2
MESH = pl.DeviceIdType.MESH
F32 = jnp.float32
BF16 = jnp.bfloat16
HIGHEST = lax.Precision.HIGHEST


def extended(block, sides, width):
    for axis, dim in sides:
        count = lax.axis_size(axis)
        forward = [(i, i + 1) for i in range(count - 1)]
        forward.append((count - 1, 0))
        backward = [(target, source) for source, target in forward]
        low = lax.ppermute(
            lax.slice_in_dim(block, block.shape[dim] - width, None, axis=dim), axis, forward
        )
        high = lax.ppermute(lax.slice_in_dim(block, 0, width, axis=dim), axis, backward)
        block = jnp.concatenate([low, block, high], axis=dim)
    return block


def outer_parts(halo_block):
    return jnp.concatenate([halo_block[0:1], halo_block[2:3], halo_block[4:5]], axis=0)


def move_requests(packed):
    swapped = lax.all_to_all(packed, "nar", split_axis=1, concat_axis=1, tiled=True)
    return outer_parts(extended(swapped, (("sub", 0),), 1))


def cg_kernel(
    ns,
    nn,
    load_hbm,
    schur_hbm,
    inverse_hbm,
    coupling_ref,
    coupling_t_ref,
    coarse_ref,
    corner_row_ref,
    meta_ref,
    send_slot_ref,
    mult,
    resid,
    schur,
    inverse,
    direction,
    image,
    jumped,
    signed,
    pick_send,
    pick_recv,
    send_buf,
    recv_buf,
    sums,
    coarse_part,
    coarse_in,
    coarse_all,
    local_sem,
    ex_send,
    ex_recv,
    sum_send,
    sum_recv,
    rs_send,
    rs_recv,
    ag_send,
    ag_recv,
):
    n = ns * nn
    sub = lax.axis_index("sub")
    nar = lax.axis_index("nar")
    me = sub * nn + nar
    rows, cols = direction.shape
    block = 2 * CAP
    band = nn * block
    owners = coarse_part.shape[0]
    tile = 256
    tiles = rows // tile

    def device(index):
        return (lax.div(index, nn), lax.rem(index, nn))

    recv_buf[0] = jnp.zeros((3 * band, cols), BF16)
    for x in range(1, recv_buf.shape[0]):
        recv_buf[x, band : band + block, :] = jnp.zeros((block, cols), BF16)

    barrier = pltpu.get_barrier_semaphore()

    def greet(i, carry):
        pl.semaphore_signal(
            barrier, inc=1, device_id=device(lax.rem(me + i, n)), device_id_type=MESH
        )
        return carry

    lax.fori_loop(1, n, greet, 0)

    load_copy = pltpu.make_async_copy(load_hbm, resid, local_sem.at[0])
    schur_copy = pltpu.make_async_copy(schur_hbm, schur, local_sem.at[1])
    inverse_copy = pltpu.make_async_copy(inverse_hbm, inverse, local_sem.at[2])
    load_copy.start()
    schur_copy.start()
    inverse_copy.start()

    def over_tiles(body):
        def step(i, carry):
            body(pl.ds(pl.multiple_of(i * tile, tile), tile))
            return carry

        lax.fori_loop(0, tiles, step, 0)

    def build_send(i, carry):
        at = pl.multiple_of(i * 128, 128)
        index = lax.broadcasted_iota(jnp.int32, (128, rows), 0) + at
        pick_send[pl.ds(at, 128), :] = jnp.where(send_slot_ref[...] == index, 1.0, 0.0).astype(BF16)
        return carry

    lax.fori_loop(0, 3 * band // 128, build_send, 0)

    def build_recv(i, carry):
        at = pl.multiple_of(i * 128, 128)
        index = lax.broadcasted_iota(jnp.int32, (128, 3 * band), 1)
        pick_recv[pl.ds(at, 128), :] = jnp.where(
            meta_ref[pl.ds(at, 128), 0:1] == index, 1.0, 0.0
        ).astype(BF16)
        return carry

    lax.fori_loop(0, rows // 128, build_recv, 0)

    corner_count = corner_row_ref.shape[1]
    coarse_size = coarse_ref.shape[1]
    corner_put = jnp.where(
        lax.broadcasted_iota(jnp.int32, (coarse_size, corner_count), 0) == corner_row_ref[...],
        1.0,
        0.0,
    ).astype(F32)

    pl.semaphore_wait(barrier, n - 1)

    def partner_copy(x, d, e, count):
        g = d * nn + e
        back = (2 - d) * nn + (nn - e) % nn
        target = (lax.rem(sub + d - 1 + ns, ns), lax.rem(nar + e, nn))
        return pltpu.make_async_remote_copy(
            src_ref=send_buf.at[pl.ds(g * block, count)],
            dst_ref=recv_buf.at[x, pl.ds(back * block, count)],
            send_sem=ex_send.at[x, g],
            recv_sem=ex_recv.at[x, back],
            device_id=target,
            device_id_type=MESH,
        )

    def arriving(x, d, e, count):
        g = d * nn + e
        return pltpu.make_async_remote_copy(
            src_ref=send_buf.at[pl.ds(g * block, count)],
            dst_ref=recv_buf.at[x, pl.ds(g * block, count)],
            send_sem=ex_send.at[x, g],
            recv_sem=ex_recv.at[x, g],
            device_id=(sub, nar),
            device_id_type=MESH,
        )

    def partners(d):
        return [e for e in range(nn) if d != 1 or e != 0]

    def exchange(x, target, count):
        copies = []
        for d in (0, 2, 1):
            send_buf[d * band : (d + 1) * band, :] = jnp.dot(
                pick_send[d * band : (d + 1) * band, :], signed[...], preferred_element_type=F32
            ).astype(BF16)
            for e in partners(d):
                copy = partner_copy(x, d, e, count)
                copy.start()
                copies.append(copy)
        for d in (1, 0, 2):
            for e in partners(d):
                arriving(x, d, e, count).wait_recv()

            def add(at):
                term = jnp.dot(
                    pick_recv[at, d * band : (d + 1) * band],
                    recv_buf[x, d * band : (d + 1) * band, :],
                    preferred_element_type=F32,
                )
                if d == 1 and target is image:
                    target[at, :] = signed[at, :].astype(F32) + term
                else:
                    target[at, :] += term

            over_tiles(add)
        for copy in copies:
            copy.wait_send()

    def all_sum(x, part):
        sums[x, 0] = part

        def send(i, carry):
            pltpu.make_async_remote_copy(
                src_ref=sums.at[x, 0],
                dst_ref=sums.at[x, n - i],
                send_sem=sum_send.at[x],
                recv_sem=sum_recv.at[x],
                device_id=device(lax.rem(me + i, n)),
                device_id_type=MESH,
            ).start()
            return carry

        lax.fori_loop(1, n, send, 0)
        every = pltpu.make_async_remote_copy(
            src_ref=sums.at[x, pl.ds(1, n - 1)],
            dst_ref=sums.at[x, pl.ds(1, n - 1)],
            send_sem=sum_send.at[x],
            recv_sem=sum_recv.at[x],
            device_id=(sub, nar),
            device_id_type=MESH,
        )
        every.wait_recv()
        total = jnp.sum(sums[x], axis=0)
        every.wait_send()
        return total

    def home_sum(first, second):
        def step(i, carry):
            at = pl.ds(pl.multiple_of(i * tile, tile), tile)
            home = meta_ref[at, 2:3] != 0
            product = jnp.where(home, first[at, :] * second[at, :], 0.0)
            return carry + jnp.sum(product, axis=0, keepdims=True)

        return lax.fori_loop(0, tiles, step, jnp.zeros((1, cols), F32))

    def jump(vector):
        def one(at):
            sign = meta_ref[at, 1:2].astype(F32)
            jumped[at, :] = (vector[at, :] * sign).astype(BF16)

        over_tiles(one)

    def precondition(x):
        jump(resid)

        def one(at):
            stiff = jnp.dot(schur[at, :], jumped[...], preferred_element_type=F32)
            sign = meta_ref[at, 1:2].astype(F32)
            signed[at, :] = (stiff.astype(BF16).astype(F32) * sign).astype(BF16)

        over_tiles(one)
        exchange(x, image, block)

    def balance(it, ref, sem, count, receive):
        whole = pltpu.make_async_remote_copy(
            src_ref=ref.at[pl.ds(0, count)],
            dst_ref=ref.at[pl.ds(0, count)],
            send_sem=sem.at[it],
            recv_sem=sem.at[it],
            device_id=(sub, nar),
            device_id_type=MESH,
        )
        if receive:
            whole.wait_recv()
        else:
            whole.wait_send()

    def flexibility(x, it):
        jump(direction)
        corner = jnp.dot(coupling_ref[...], jumped[...], preferred_element_type=F32)
        part = jnp.dot(corner_put, corner, precision=HIGHEST, preferred_element_type=F32)
        coarse_part[...] = part.reshape(owners, 8, cols)

        def scatter(i, carry):
            t = lax.rem(me + i, n)

            @pl.when(t < owners)
            def _():
                pltpu.make_async_remote_copy(
                    src_ref=coarse_part.at[t],
                    dst_ref=coarse_in.at[it, n - i],
                    send_sem=rs_send.at[it],
                    recv_sem=rs_recv.at[it],
                    device_id=device(t),
                    device_id_type=MESH,
                ).start()

            return carry

        lax.fori_loop(1, n, scatter, 0)

        def product(i, carry):
            at = pl.ds(pl.multiple_of(i * tile, tile), tile)
            image[at, :] = jnp.dot(inverse[at, :], jumped[...], preferred_element_type=F32)
            return carry

        lax.fori_loop(0, tiles // 2, product, 0)

        @pl.when(me < owners)
        def _():
            coarse_in[it, 0] = coarse_part[me]
            balance_in = pltpu.make_async_remote_copy(
                src_ref=coarse_in.at[it, pl.ds(1, n - 1)],
                dst_ref=coarse_in.at[it, pl.ds(1, n - 1)],
                send_sem=rs_send.at[it],
                recv_sem=rs_recv.at[it],
                device_id=(sub, nar),
                device_id_type=MESH,
            )
            balance_in.wait_recv()
            coarse_all[it, me] = jnp.sum(coarse_in[it], axis=0)

            def spread(i, carry):
                pltpu.make_async_remote_copy(
                    src_ref=coarse_all.at[it, me],
                    dst_ref=coarse_all.at[it, me],
                    send_sem=ag_send.at[it],
                    recv_sem=ag_recv.at[it],
                    device_id=device(lax.rem(me + i, n)),
                    device_id_type=MESH,
                ).start()
                return carry

            lax.fori_loop(1, n, spread, 0)

        lax.fori_loop(tiles // 2, tiles, product, 0)

        @pl.when(me < owners)
        def _():
            balance(it, coarse_part, rs_send, owners - 1, False)
            balance(it, coarse_all.at[it], ag_recv, owners - 1, True)

        @pl.when(me >= owners)
        def _():
            balance(it, coarse_part, rs_send, owners, False)
            balance(it, coarse_all.at[it], ag_recv, owners, True)

        load = coarse_all[it].reshape(owners * 8, cols)
        answer = jnp.dot(
            coarse_ref[...], load, precision=HIGHEST, preferred_element_type=F32
        ).astype(BF16)

        def finish(at):
            back = jnp.dot(coupling_t_ref[at, :], answer, preferred_element_type=F32)
            sign = meta_ref[at, 1:2].astype(F32)
            summed = (image[at, :] + back).astype(BF16).astype(F32)
            signed[at, :] = (summed * sign).astype(BF16)

        over_tiles(finish)
        exchange(x, image, block)

        @pl.when(me < owners)
        def _():
            balance(it, coarse_in.at[it], ag_send, n - 1, False)

    load_copy.wait()

    def round_load(at):
        signed[at, :] = resid[at, :].astype(BF16)

    over_tiles(round_load)
    exchange(0, resid, CAP)

    schur_copy.wait()
    precondition(1)
    energy = all_sum(0, home_sum(resid, image))

    def first_direction(at):
        direction[at, :] = image[at, :]
        mult[at, :] = jnp.zeros((tile, cols), F32)

    over_tiles(first_direction)
    inverse_copy.wait()
    for it in range(ITERS):
        flexibility(2 * it + 2, it)
        step_size = energy / all_sum(2 * it + 1, home_sum(direction, image))

        def advance(at):
            mult[at, :] += step_size * direction[at, :]
            resid[at, :] -= step_size * image[at, :]

        over_tiles(advance)
        if it + 1 < ITERS:
            precondition(2 * it + 3)
            later = all_sum(2 * it + 2, home_sum(resid, image))
            ratio = later / energy

            def turn(at):
                direction[at, :] = image[at, :] + ratio * direction[at, :]

            over_tiles(turn)
            energy = later


def body(
    remainder_inverse,
    dirichlet_schur,
    corner_coupling,
    coarse_inverse,
    jump_load,
    dof_multiplier,
    dof_sign,
    corner_index,
):
    coupling = corner_coupling[0]
    targets = dof_multiplier[0]
    sign_list = dof_sign[0]
    owned_rows, columns = jump_load.shape
    coarse_size = coarse_inverse.shape[0]
    local_count = targets.shape[0]
    ns = lax.axis_size("sub")
    nn = lax.axis_size("nar")
    n = ns * nn
    sub = lax.axis_index("sub")
    nar = lax.axis_index("nar")
    me = sub * nn + nar
    slot_count = 3 * nn * CAP
    holder = targets // owned_rows
    linked = sign_list != 0
    at_home = linked & (holder == me)
    remote = linked & (holder != me)
    offset = (holder // nn - sub) % ns
    sub_band = jnp.where(offset == 0, 1, jnp.where(offset == 1, 2, 0))
    places = jnp.arange(local_count, dtype=jnp.int32)
    peer = jnp.where(remote, holder, -1)
    earlier = (holder[:, None] == peer[None, :]) & (places[None, :] < places[:, None])
    rank = jnp.sum(earlier.astype(jnp.int32), axis=1)
    asked = jnp.where(remote, (sub_band * nn + holder % nn) * CAP + rank, -1)
    row = targets - holder * owned_rows
    slots = jnp.arange(slot_count, dtype=jnp.int32)
    requests = jnp.sum(jnp.where(asked[None, :] == slots[:, None], row[None, :] + 1, 0), axis=1) - 1
    wanted = move_requests(requests.reshape(3, nn, CAP)).reshape(slot_count)
    own_row = jnp.where(at_home, row, -2)
    home_slot = (
        (slots // (nn * CAP) * nn + (slots // CAP % nn - nar) % nn) * (2 * CAP)
        + CAP
        + slots % CAP
    )
    at_home_slot = jnp.sum(
        jnp.where(own_row[:, None] == wanted[None, :], home_slot[None, :], 0), axis=1
    )
    remote_slot = (sub_band * nn + (holder % nn - nar) % nn) * (2 * CAP) + rank
    slot = jnp.where(at_home, at_home_slot, jnp.where(remote, remote_slot, -1))
    send_slot = jnp.where(at_home, slot - CAP, jnp.where(remote, slot + CAP, -1))
    meta = jnp.stack([slot, sign_list, at_home.astype(jnp.int32), own_row], axis=1)
    home_load = jnp.where(at_home[:, None], jump_load[jnp.where(at_home, row, 0)], 0.0)

    vmem = pl.BlockSpec(memory_space=pltpu.VMEM)
    hbm = pl.BlockSpec(memory_space=pl.ANY)
    slots_all = 6 * nn * CAP
    owners = coarse_size // 8
    dma = pltpu.SemaphoreType.DMA
    exchanges = 2 * ITERS + 1
    state = jax.ShapeDtypeStruct((local_count, columns), F32)
    mult, resid = pl.pallas_call(
        functools.partial(cg_kernel, ns, nn),
        out_shape=(state, state),
        in_specs=[hbm] * 3 + [vmem] * 6,
        out_specs=(vmem, vmem),
        scratch_shapes=[
            pltpu.VMEM((local_count, local_count), BF16),
            pltpu.VMEM((local_count, local_count), BF16),
            pltpu.VMEM((local_count, columns), F32),
            pltpu.VMEM((local_count, columns), F32),
            pltpu.VMEM((local_count, columns), BF16),
            pltpu.VMEM((local_count, columns), BF16),
            pltpu.VMEM((slots_all, local_count), BF16),
            pltpu.VMEM((local_count, slots_all), BF16),
            pltpu.VMEM((slots_all, columns), BF16),
            pltpu.VMEM((exchanges, slots_all, columns), BF16),
            pltpu.VMEM((2 * ITERS, n, 1, columns), F32),
            pltpu.VMEM((owners, 8, columns), F32),
            pltpu.VMEM((ITERS, n, 8, columns), F32),
            pltpu.VMEM((ITERS, owners, 8, columns), F32),
            dma((3,)),
            dma((exchanges, 3 * nn)),
            dma((exchanges, 3 * nn)),
            dma((2 * ITERS,)),
            dma((2 * ITERS,)),
            dma((ITERS,)),
            dma((ITERS,)),
            dma((ITERS,)),
            dma((ITERS,)),
        ],
        compiler_params=pltpu.CompilerParams(
            collective_id=0, has_side_effects=True, vmem_limit_bytes=60 * 1024 * 1024
        ),
    )(
        home_load,
        dirichlet_schur[0],
        remainder_inverse[0],
        coupling,
        coupling.T,
        coarse_inverse[corner_index[0]],
        corner_index.reshape(1, -1),
        meta,
        send_slot.reshape(1, -1),
    )
    owned = jnp.arange(owned_rows, dtype=jnp.int32)
    home_places = jnp.sum(
        jnp.where(own_row[None, :] == owned[:, None], places[None, :], 0), axis=1
    )
    return mult[home_places], resid[home_places]


def solution(mesh):
    placed = (
        P(("sub", "nar"), None, None),
        P(("sub", "nar"), None, None),
        P(("sub", "nar"), None, None),
        P(),
        P(("sub", "nar"), None),
        P(("sub", "nar"), None),
        P(("sub", "nar"), None),
        P(("sub", "nar"), None),
    )
    return jax.shard_map(
        body,
        mesh=mesh,
        in_specs=placed,
        out_specs=(P(("sub", "nar"), None), P(("sub", "nar"), None)),
        check_vma=False,
    )
```

```python
import functools

import jax
import jax.numpy as jnp
from jax import lax
from jax.experimental import pallas as pl
from jax.experimental.pallas import tpu as pltpu
from jax.sharding import PartitionSpec as P

CAP = 96
ITERS = 2
MESH = pl.DeviceIdType.MESH
F32 = jnp.float32
BF16 = jnp.bfloat16
HIGHEST = lax.Precision.HIGHEST


def extended(block, sides, width):
    for axis, dim in sides:
        count = lax.axis_size(axis)
        forward = [(i, i + 1) for i in range(count - 1)]
        forward.append((count - 1, 0))
        backward = [(target, source) for source, target in forward]
        low = lax.ppermute(
            lax.slice_in_dim(block, block.shape[dim] - width, None, axis=dim), axis, forward
        )
        high = lax.ppermute(lax.slice_in_dim(block, 0, width, axis=dim), axis, backward)
        block = jnp.concatenate([low, block, high], axis=dim)
    return block


def outer_parts(halo_block):
    return jnp.concatenate([halo_block[0:1], halo_block[2:3], halo_block[4:5]], axis=0)


def move_requests(packed):
    swapped = lax.all_to_all(packed, "nar", split_axis=1, concat_axis=1, tiled=True)
    return outer_parts(extended(swapped, (("sub", 0),), 1))


def cg_kernel(
    ns,
    nn,
    load_ref,
    schur_hbm,
    inverse_hbm,
    coupling_ref,
    coupling_t_ref,
    coarse_ref,
    corner_row_ref,
    meta_ref,
    send_slot_ref,
    own_row_ref,
    mult_out,
    resid_out,
    mult,
    resid,
    schur,
    inverse,
    direction,
    image,
    jumped,
    signed,
    pick_send,
    pick_recv,
    send_buf,
    recv_buf,
    sums,
    coarse_part,
    coarse_in,
    coarse_all,
    local_sem,
    ex_send,
    ex_recv,
    sum_send,
    sum_recv,
    rs_send,
    rs_recv,
    ag_send,
    ag_recv,
):
    n = ns * nn
    sub = lax.axis_index("sub")
    nar = lax.axis_index("nar")
    me = sub * nn + nar
    rows, cols = direction.shape
    block = 2 * CAP
    band = nn * block
    owners = coarse_part.shape[0]
    tile = 256
    tiles = rows // tile

    def device(index):
        return (lax.div(index, nn), lax.rem(index, nn))

    recv_buf[0] = jnp.zeros((3 * band, cols), BF16)
    recv_buf[1, band : band + block, :] = jnp.zeros((block, cols), BF16)

    barrier = pltpu.get_barrier_semaphore()

    def greet(i, carry):
        pl.semaphore_signal(
            barrier, inc=1, device_id=device(lax.rem(me + i, n)), device_id_type=MESH
        )
        return carry

    lax.fori_loop(1, n, greet, 0)

    schur_copy = pltpu.make_async_copy(schur_hbm, schur, local_sem.at[1])
    inverse_copy = pltpu.make_async_copy(inverse_hbm, inverse, local_sem.at[2])
    schur_copy.start()
    inverse_copy.start()

    def over_tiles(body):
        def step(i, carry):
            body(pl.ds(pl.multiple_of(i * tile, tile), tile))
            return carry

        lax.fori_loop(0, tiles, step, 0)

    def build_send(i, carry):
        at = pl.multiple_of(i * 128, 128)
        index = lax.broadcasted_iota(jnp.int32, (128, rows), 0) + at
        pick_send[pl.ds(at, 128), :] = jnp.where(send_slot_ref[...] == index, 1.0, 0.0).astype(BF16)
        return carry

    lax.fori_loop(0, 3 * band // 128, build_send, 0)

    def build_recv(i, carry):
        at = pl.multiple_of(i * 128, 128)
        index = lax.broadcasted_iota(jnp.int32, (128, 3 * band), 1)
        pick_recv[pl.ds(at, 128), :] = jnp.where(
            meta_ref[pl.ds(at, 128), 0:1] == index, 1.0, 0.0
        ).astype(BF16)
        return carry

    lax.fori_loop(0, rows // 128, build_recv, 0)

    corner_count = corner_row_ref.shape[1]
    coarse_size = coarse_ref.shape[1]
    corner_put = jnp.where(
        lax.broadcasted_iota(jnp.int32, (coarse_size, corner_count), 0) == corner_row_ref[...],
        1.0,
        0.0,
    ).astype(F32)

    pl.semaphore_wait(barrier, n - 1)

    def partner_copy(x, d, e, count):
        g = d * nn + e
        back = (2 - d) * nn + (nn - e) % nn
        target = (lax.rem(sub + d - 1 + ns, ns), lax.rem(nar + e, nn))
        return pltpu.make_async_remote_copy(
            src_ref=send_buf.at[pl.ds(g * block, count)],
            dst_ref=recv_buf.at[x % 2, pl.ds(back * block, count)],
            send_sem=ex_send.at[x, g],
            recv_sem=ex_recv.at[x, back],
            device_id=target,
            device_id_type=MESH,
        )

    def arriving(x, d, e, count):
        g = d * nn + e
        return pltpu.make_async_remote_copy(
            src_ref=send_buf.at[pl.ds(g * block, count)],
            dst_ref=recv_buf.at[x % 2, pl.ds(g * block, count)],
            send_sem=ex_send.at[x, g],
            recv_sem=ex_recv.at[x, g],
            device_id=(sub, nar),
            device_id_type=MESH,
        )

    def partners(d):
        return [e for e in range(nn) if d != 1 or e != 0]

    def exchange(x, target, count, part=None, meanwhile=None):
        copies = []
        for d in (0, 2, 1):
            send_buf[d * band : (d + 1) * band, :] = jnp.dot(
                pick_send[d * band : (d + 1) * band, :], signed[...], preferred_element_type=F32
            ).astype(BF16)
            for e in partners(d):
                copy = partner_copy(x, d, e, count)
                copy.start()
                copies.append(copy)
            if d == 0 and part is not None:
                send_sums(x - 1, part)
        if meanwhile is not None:
            meanwhile()
        for d in (1, 0, 2):
            for e in partners(d):
                arriving(x, d, e, count).wait_recv()

            def add(at):
                term = jnp.dot(
                    pick_recv[at, d * band : (d + 1) * band],
                    recv_buf[x % 2, d * band : (d + 1) * band, :],
                    preferred_element_type=F32,
                )
                if d == 1 and target is image:
                    target[at, :] = signed[at, :].astype(F32) + term
                else:
                    target[at, :] += term

            over_tiles(add)
        for copy in copies:
            copy.wait_send()

    def send_sums(x, part):
        sums[x, 0] = part

        def send(i, carry):
            pltpu.make_async_remote_copy(
                src_ref=sums.at[x, 0],
                dst_ref=sums.at[x, n - i],
                send_sem=sum_send.at[x],
                recv_sem=sum_recv.at[x],
                device_id=device(lax.rem(me + i, n)),
                device_id_type=MESH,
            ).start()
            return carry

        lax.fori_loop(1, n, send, 0)

    def all_sum(x):
        every = pltpu.make_async_remote_copy(
            src_ref=sums.at[x, pl.ds(1, n - 1)],
            dst_ref=sums.at[x, pl.ds(1, n - 1)],
            send_sem=sum_send.at[x],
            recv_sem=sum_recv.at[x],
            device_id=(sub, nar),
            device_id_type=MESH,
        )
        every.wait_recv()
        total = jnp.sum(sums[x], axis=0)
        every.wait_send()
        return total

    def share(vector):
        def step(i, carry):
            at = pl.ds(pl.multiple_of(i * tile, tile), tile)
            product = vector[at, :] * signed[at, :].astype(F32)
            return carry + jnp.sum(product, axis=0, keepdims=True)

        return lax.fori_loop(0, tiles, step, jnp.zeros((1, cols), F32))

    def jump(vector):
        def one(at):
            sign = meta_ref[at, 1:2].astype(F32)
            jumped[at, :] = (vector[at, :] * sign).astype(BF16)

        over_tiles(one)

    def precondition(x):
        jump(resid)

        def one(at):
            stiff = jnp.dot(schur[at, :], jumped[...], preferred_element_type=F32)
            sign = meta_ref[at, 1:2].astype(F32)
            signed[at, :] = (stiff.astype(BF16).astype(F32) * sign).astype(BF16)

        over_tiles(one)
        exchange(x, image, block, share(resid))

    def balance(it, ref, sem, count, receive):
        whole = pltpu.make_async_remote_copy(
            src_ref=ref.at[pl.ds(0, count)],
            dst_ref=ref.at[pl.ds(0, count)],
            send_sem=sem.at[it],
            recv_sem=sem.at[it],
            device_id=(sub, nar),
            device_id_type=MESH,
        )
        if receive:
            whole.wait_recv()
        else:
            whole.wait_send()

    def flexibility(x, it, meanwhile=None):
        jump(direction)
        corner = jnp.dot(coupling_ref[...], jumped[...], preferred_element_type=F32)
        part = jnp.dot(corner_put, corner, precision=HIGHEST, preferred_element_type=F32)
        coarse_part[...] = part.reshape(owners, 8, cols)

        def scatter(i, carry):
            t = lax.rem(me + i, n)

            @pl.when(t < owners)
            def _():
                pltpu.make_async_remote_copy(
                    src_ref=coarse_part.at[t],
                    dst_ref=coarse_in.at[it, n - i],
                    send_sem=rs_send.at[it],
                    recv_sem=rs_recv.at[it],
                    device_id=device(t),
                    device_id_type=MESH,
                ).start()

            return carry

        lax.fori_loop(1, n, scatter, 0)

        def product(i, carry):
            at = pl.ds(pl.multiple_of(i * tile, tile), tile)
            image[at, :] = jnp.dot(inverse[at, :], jumped[...], preferred_element_type=F32)
            return carry

        lax.fori_loop(0, tiles // 2, product, 0)

        @pl.when(me < owners)
        def _():
            coarse_in[it, 0] = coarse_part[me]
            balance_in = pltpu.make_async_remote_copy(
                src_ref=coarse_in.at[it, pl.ds(1, n - 1)],
                dst_ref=coarse_in.at[it, pl.ds(1, n - 1)],
                send_sem=rs_send.at[it],
                recv_sem=rs_recv.at[it],
                device_id=(sub, nar),
                device_id_type=MESH,
            )
            balance_in.wait_recv()
            coarse_all[it, me] = jnp.sum(coarse_in[it], axis=0)

            def spread(i, carry):
                pltpu.make_async_remote_copy(
                    src_ref=coarse_all.at[it, me],
                    dst_ref=coarse_all.at[it, me],
                    send_sem=ag_send.at[it],
                    recv_sem=ag_recv.at[it],
                    device_id=device(lax.rem(me + i, n)),
                    device_id_type=MESH,
                ).start()
                return carry

            lax.fori_loop(1, n, spread, 0)

        lax.fori_loop(tiles // 2, tiles, product, 0)

        @pl.when(me < owners)
        def _():
            balance(it, coarse_part, rs_send, owners - 1, False)
            balance(it, coarse_all.at[it], ag_recv, owners - 1, True)

        @pl.when(me >= owners)
        def _():
            balance(it, coarse_part, rs_send, owners, False)
            balance(it, coarse_all.at[it], ag_recv, owners, True)

        load = coarse_all[it].reshape(owners * 8, cols)
        answer = jnp.dot(
            coarse_ref[...], load, precision=HIGHEST, preferred_element_type=F32
        ).astype(BF16)

        def finish(at):
            back = jnp.dot(coupling_t_ref[at, :], answer, preferred_element_type=F32)
            sign = meta_ref[at, 1:2].astype(F32)
            summed = (image[at, :] + back).astype(BF16).astype(F32)
            signed[at, :] = (summed * sign).astype(BF16)

        over_tiles(finish)
        exchange(x, image, block, share(direction), meanwhile)

        @pl.when(me < owners)
        def _():
            balance(it, coarse_in.at[it], ag_send, n - 1, False)

    def split(values):
        high = values.astype(BF16)
        rest = values - high.astype(F32)
        middle = rest.astype(BF16)
        return jnp.concatenate([high, middle, (rest - middle.astype(F32)).astype(BF16)], axis=1)

    def joined(parts):
        return parts[:, :cols] + parts[:, cols : 2 * cols] + parts[:, 2 * cols :]

    owned = mult_out.shape[0]
    out_tile = 120 if owned % 120 == 0 else 8

    def home_rows(vector, put):
        def keep(at):
            schur[at, : 3 * cols] = split(vector[at, :])

        over_tiles(keep)

        def pick(i, carry):
            at = pl.multiple_of(i * out_tile, out_tile)
            index = lax.broadcasted_iota(jnp.int32, (out_tile, rows), 0) + at
            one_hot = jnp.where(own_row_ref[...] == index, 1.0, 0.0).astype(BF16)
            put(
                pl.ds(at, out_tile),
                joined(jnp.dot(one_hot, schur[:, : 3 * cols], preferred_element_type=F32)),
            )
            return carry

        lax.fori_loop(0, owned // out_tile, pick, 0)

    def put_mult(at, values):
        mult_out[at, :] = values

    def put_resid(at, values):
        resid_out[at, :] = values

    def put_direction(at, values):
        mult[at, :] = values

    def early_rows():
        home_rows(mult, put_mult)
        home_rows(resid, put_resid)
        home_rows(direction, put_direction)

    load_parts = split(load_ref[...])

    def take_load(at):
        index = lax.broadcasted_iota(jnp.int32, (tile, owned), 1)
        one_hot = jnp.where(meta_ref[at, 3:4] == index, 1.0, 0.0).astype(BF16)
        resid[at, :] = joined(jnp.dot(one_hot, load_parts, preferred_element_type=F32))
        signed[at, :] = resid[at, :].astype(BF16)

    over_tiles(take_load)
    exchange(0, resid, CAP)

    schur_copy.wait()
    precondition(1)
    energy = all_sum(0)

    def first_direction(at):
        direction[at, :] = image[at, :]
        mult[at, :] = jnp.zeros((tile, cols), F32)

    over_tiles(first_direction)
    inverse_copy.wait()
    for it in range(ITERS):
        last = it + 1 == ITERS
        flexibility(2 * it + 2, it, early_rows if last else None)
        if last:
            step_size = energy / all_sum(2 * it + 1)
            mult_out[...] += step_size * mult[:owned, :]

            def put_image(at, values):
                resid_out[at, :] -= step_size * values

            home_rows(image, put_image)
            break
        step_size = energy / all_sum(2 * it + 1)

        def advance(at):
            mult[at, :] += step_size * direction[at, :]
            resid[at, :] -= step_size * image[at, :]

        over_tiles(advance)
        if it + 1 < ITERS:
            precondition(2 * it + 3)
            later = all_sum(2 * it + 2)
            ratio = later / energy

            def turn(at):
                direction[at, :] = image[at, :] + ratio * direction[at, :]

            over_tiles(turn)
            energy = later


def body(
    remainder_inverse,
    dirichlet_schur,
    corner_coupling,
    coarse_inverse,
    jump_load,
    dof_multiplier,
    dof_sign,
    corner_index,
):
    coupling = corner_coupling[0]
    targets = dof_multiplier[0]
    sign_list = dof_sign[0]
    owned_rows, columns = jump_load.shape
    coarse_size = coarse_inverse.shape[0]
    local_count = targets.shape[0]
    ns = lax.axis_size("sub")
    nn = lax.axis_size("nar")
    n = ns * nn
    sub = lax.axis_index("sub")
    nar = lax.axis_index("nar")
    me = sub * nn + nar
    slot_count = 3 * nn * CAP
    holder = targets // owned_rows
    linked = sign_list != 0
    at_home = linked & (holder == me)
    remote = linked & (holder != me)
    offset = (holder // nn - sub) % ns
    sub_band = jnp.where(offset == 0, 1, jnp.where(offset == 1, 2, 0))
    places = jnp.arange(local_count, dtype=jnp.int32)
    peer = jnp.where(remote, holder, -1)
    earlier = (holder[:, None] == peer[None, :]) & (places[None, :] < places[:, None])
    rank = jnp.sum(earlier.astype(jnp.int32), axis=1)
    asked = jnp.where(remote, (sub_band * nn + holder % nn) * CAP + rank, -1)
    row = targets - holder * owned_rows
    slots = jnp.arange(slot_count, dtype=jnp.int32)
    requests = jnp.sum(jnp.where(asked[None, :] == slots[:, None], row[None, :] + 1, 0), axis=1) - 1
    wanted = move_requests(requests.reshape(3, nn, CAP)).reshape(slot_count)
    own_row = jnp.where(at_home, row, -2)
    home_slot = (
        (slots // (nn * CAP) * nn + (slots // CAP % nn - nar) % nn) * (2 * CAP)
        + CAP
        + slots % CAP
    )
    at_home_slot = jnp.sum(
        jnp.where(own_row[:, None] == wanted[None, :], home_slot[None, :], 0), axis=1
    )
    remote_slot = (sub_band * nn + (holder % nn - nar) % nn) * (2 * CAP) + rank
    slot = jnp.where(at_home, at_home_slot, jnp.where(remote, remote_slot, -1))
    send_slot = jnp.where(at_home, slot - CAP, jnp.where(remote, slot + CAP, -1))
    meta = jnp.stack([slot, sign_list, at_home.astype(jnp.int32), own_row], axis=1)

    vmem = pl.BlockSpec(memory_space=pltpu.VMEM)
    hbm = pl.BlockSpec(memory_space=pl.ANY)
    slots_all = 6 * nn * CAP
    owners = coarse_size // 8
    dma = pltpu.SemaphoreType.DMA
    exchanges = 2 * ITERS + 1
    state = jax.ShapeDtypeStruct((owned_rows, columns), F32)
    return pl.pallas_call(
        functools.partial(cg_kernel, ns, nn),
        out_shape=(state, state),
        in_specs=[vmem] + [hbm] * 2 + [vmem] * 7,
        out_specs=(vmem, vmem),
        scratch_shapes=[
            pltpu.VMEM((local_count, columns), F32),
            pltpu.VMEM((local_count, columns), F32),
            pltpu.VMEM((local_count, local_count), BF16),
            pltpu.VMEM((local_count, local_count), BF16),
            pltpu.VMEM((local_count, columns), F32),
            pltpu.VMEM((local_count, columns), F32),
            pltpu.VMEM((local_count, columns), BF16),
            pltpu.VMEM((local_count, columns), BF16),
            pltpu.VMEM((slots_all, local_count), BF16),
            pltpu.VMEM((local_count, slots_all), BF16),
            pltpu.VMEM((slots_all, columns), BF16),
            pltpu.VMEM((2, slots_all, columns), BF16),
            pltpu.VMEM((2 * ITERS, n, 1, columns), F32),
            pltpu.VMEM((owners, 8, columns), F32),
            pltpu.VMEM((ITERS, n, 8, columns), F32),
            pltpu.VMEM((ITERS, owners, 8, columns), F32),
            dma((3,)),
            dma((exchanges, 3 * nn)),
            dma((exchanges, 3 * nn)),
            dma((2 * ITERS,)),
            dma((2 * ITERS,)),
            dma((ITERS,)),
            dma((ITERS,)),
            dma((ITERS,)),
            dma((ITERS,)),
        ],
        compiler_params=pltpu.CompilerParams(
            collective_id=0, has_side_effects=True, vmem_limit_bytes=60 * 1024 * 1024
        ),
    )(
        jump_load,
        dirichlet_schur[0],
        remainder_inverse[0],
        coupling,
        coupling.T,
        coarse_inverse[corner_index[0]],
        corner_index.reshape(1, -1),
        meta,
        send_slot.reshape(1, -1),
        own_row.reshape(1, -1),
    )


def solution(mesh):
    placed = (
        P(("sub", "nar"), None, None),
        P(("sub", "nar"), None, None),
        P(("sub", "nar"), None, None),
        P(),
        P(("sub", "nar"), None),
        P(("sub", "nar"), None),
        P(("sub", "nar"), None),
        P(("sub", "nar"), None),
    )
    return jax.shard_map(
        body,
        mesh=mesh,
        in_specs=placed,
        out_specs=(P(("sub", "nar"), None), P(("sub", "nar"), None)),
        check_vma=False,
    )
```
